32 devices in a mesh: grp: 4 (over y, x), dev: 8 (over z, core).
Axes of the slice: x: 2, y: 2, z: 4, core: 2. Of those that a mesh axis runs over, the one named last changes fastest.
Arguments:
- canvas: bfloat16 [256, 1024, 256], P('grp', 'dev'), may hold values from -6 to 6
- conv_weight: bfloat16 [2304, 256], replicated, may hold values from -0.125 to 0.125
- conv_bias: float32 [256], replicated, may hold values from -3 to 3
- score_weight: float32 [256], replicated, may hold values from -0.75 to 0.75
- tile_tokens: bfloat16 [1024, 24, 3200], P(('grp', 'dev')), may hold values from -6 to 6
- tile_cell: int32 [4, 256], P('grp', 'dev'), may hold values from 0 to 8191
- tile_count: int32 [4, 8], P('grp'), may hold values from 1 to 32, 64 in all within a row
- holder_order: int32 [4, 8], P('grp'), may hold values from 0 to 7, each once within a row
- tile_image: int32 [4, 64], P('grp'), may hold values from 0 to 31, never falling along the last dimension, each value on 1 to 9 neighbouring positions
- ln_gain: float32 [3200], replicated, may hold values from 0.25 to 1.75
- qkv_weight: bfloat16 [3200, 4992], P(('grp', 'dev')), may hold values from -2 to 2
Outputs:
- score_map: float32 [256, 1024], P('grp', 'dev')
- attended: bfloat16 [6144, 1664], P(('grp', 'dev'))
The draws below stay inside these ranges and needn't reach their ends.
Inputs may be any that keep to these rules, and one draw needn't show every extreme that they name: `tile_count`: the counts of one group add up to 64; in each group one device holds exactly 32. `tile_image`: ids never fall along a group's held tiles; each image has 1 to 9 tiles and one has exactly 9.
All inputs are finite; a program needn't handle non-finite values.
Results may differ from the reference program's by a relative error of at most 0.012.
Values may be sent and summed in bfloat16 or wider, within the bound.
A program may use at most 192 MiB of HBM per device.

```python
import math
import jax
import jax.numpy as jnp
import numpy as np
from jax import lax

D = 3200
HD = 128
HEADS = 13
CIN = 256
CHID = 256
CH = 64
CW = 128
TT = 24
MT = 8
SLOTS = 32
HW = 1664
IMAGES = 32
CANVAS_H = 256
CANVAS_W = 1024
TILES = 1024
N_GRP = 4
N_DEV = 8


def draw_tile_tokens(key, part):
    shape = (TILES, TT, D)
    values = jnp.clip(jax.random.normal(key, shape, jnp.float32), -6.0, 6.0)
    return values.astype(jnp.bfloat16)


def draw_qkv_weight(key, part):
    scale = 1.0 / math.sqrt(D)
    whole = jnp.clip(jax.random.normal(key, (D, 3 * HW), jnp.float32), -6.0, 6.0) * scale
    return whole.astype(jnp.bfloat16)


def with_ends(values, key, smallest, largest):
    shape = values.shape
    index_at = [jax.random.randint(jax.random.fold_in(key, axis), (), 0, shape[axis]) for axis in range(len(shape))]
    values = values.at[tuple(index_at)].set(smallest)
    longest = shape.index(max(shape))
    index_at[longest] = (index_at[longest] + 1) % shape[longest]
    return values.at[tuple(index_at)].set(largest)


def block_scale(key, shape, shards, low, high):
    level, own = 1.0, jax.random.fold_in(key, 6)
    for dim, shards_of in shards:
        draws = jnp.exp(jax.random.uniform(jax.random.fold_in(own, dim), (shards_of,), jnp.float32, low / len(shards), high / len(shards)))
        level = level * jnp.repeat(draws, shape[dim] // shards_of).reshape([-1 if axis == dim else 1 for axis in range(len(shape))])
    return level


def split_up(number_of, total, reach, skew):
    weights = [(1 << 20) // math.isqrt(grade ** skew) + 1 for grade in range(2, number_of + 1)]
    spare, given = total - reach - (number_of - 1), [1] * (number_of - 1)
    while spare > 0:
        movable = [i for i in range(number_of - 1) if given[i] < reach]
        whole, budget = sum([weights[i] for i in movable]), spare
        for i in movable:
            more = min(reach - given[i], max(1, budget * weights[i] // whole), spare)
            given[i] = given[i] + more
            spare = spare - more
    return np.array([reach] + given)


def uneven_parts(rng, number_of, total, most, skew):
    if number_of == 2:
        one = jax.random.randint(rng, (), max(1, total - most), min(most, total - 1) + 1)
        return jnp.stack([one, total - one])
    lengths = jnp.asarray(split_up(number_of, total, most, skew), jnp.int32)
    pairs = (number_of - 1) // 2
    giver, taker = lengths[1:1 + 2 * pairs:2], lengths[2:2 + 2 * pairs:2]
    slack = jnp.minimum(giver - 1, most - taker)
    passed = jax.random.randint(jax.random.fold_in(rng, 1), (pairs,), 0, 1 << 20) % (slack + 1)
    lengths = lengths.at[1:1 + 2 * pairs:2].set(giver - passed).at[2:2 + 2 * pairs:2].set(taker + passed)
    return lengths[jax.random.permutation(jax.random.fold_in(rng, 2), number_of)]


def scatter_about(key, extent, deviation, limit, cuts=(), held_as=jnp.bfloat16):
    drawn = deviation * jax.random.normal(key, extent, jnp.float32)
    if cuts:
        drawn = drawn * block_scale(key, extent, cuts, -0.22, 0.18)
    return jnp.clip(drawn, -limit, limit).astype(held_as)


def setup_inputs(seed: int = 0) -> dict:
    key_list = jax.random.split(jax.random.key(seed), 12)
    canvas = scatter_about(key_list[0], (CANVAS_H, CANVAS_W, CIN), 1.0, 6.0, ((0, 4), (1, 8)))
    conv_weight = scatter_about(key_list[1], (9 * CIN, CHID), (9 * CIN) ** -0.5, 0.125)
    conv_bias = scatter_about(key_list[2], (CHID,), 0.5, 3.0, (), jnp.float32)
    score_weight = scatter_about(key_list[3], (CHID,), (CHID // 4) ** -0.5, 0.75, (), jnp.float32)
    tile_tokens = draw_tile_tokens(jax.random.fold_in(key_list[11], 71), 0)
    tile_cell = with_ends(jax.random.randint(key_list[5], (N_GRP, N_DEV * SLOTS), 0, CH * CW), jax.random.fold_in(key_list[5], 1), 0, (CH * CW) - 1).astype(jnp.int32)
    tile_count = jax.vmap(lambda own: uneven_parts(own, N_DEV, MT * N_DEV, SLOTS, 2))(jax.random.split(key_list[6], N_GRP)).reshape((N_GRP, N_DEV)).astype(jnp.int32)
    holder_order = jax.vmap(lambda own: jax.random.permutation(own, N_DEV))(jax.random.split(key_list[7], N_GRP)).reshape((N_GRP, N_DEV)).astype(jnp.int32)
    tile_image = jax.vmap(lambda own: jnp.searchsorted(jnp.cumsum(uneven_parts(own, IMAGES, N_DEV * MT, MT + 1, 0)), jnp.arange(N_DEV * MT), side="right"))(jax.random.split(key_list[8], N_GRP)).reshape((N_GRP, N_DEV * MT)).astype(jnp.int32)
    ln_gain = jnp.clip(1.0 + 0.15 * jax.random.normal(key_list[9], (D,), jnp.float32), 0.25, 1.75)
    qkv_weight = draw_qkv_weight(jax.random.fold_in(key_list[11], 71), 0)
    return {"canvas": canvas, "conv_weight": conv_weight, "conv_bias": conv_bias, "score_weight": score_weight, "tile_tokens": tile_tokens, "tile_cell": tile_cell, "tile_count": tile_count, "holder_order": holder_order, "tile_image": tile_image, "ln_gain": ln_gain, "qkv_weight": qkv_weight}


def layer_norm(rows, gain):
    values = rows.astype(jnp.float32)
    center = lax.optimization_barrier(jnp.mean(values, axis=1, keepdims=True))
    spread = lax.optimization_barrier(jnp.mean(jnp.square(values - center), axis=1, keepdims=True))
    return ((values - center) * lax.rsqrt(spread + 1e-06) * gain).astype(jnp.bfloat16)

def conv_scores(padded, conv_weight, conv_bias, score_weight, height, breadth):
    channels = padded.shape[2]
    summed = jnp.zeros((height * breadth, conv_weight.shape[1]), jnp.float32)
    for row_off in range(3):
        for col_off in range(3):
            window = padded[row_off:row_off + height, col_off:col_off + breadth].reshape(height * breadth, channels)
            offset = (row_off * 3 + col_off) * channels
            summed = summed + jnp.dot(window, conv_weight[offset:offset + channels], preferred_element_type=jnp.float32)
    hidden = jax.nn.gelu(summed + conv_bias)
    return jnp.dot(hidden, score_weight, precision=lax.Precision.HIGHEST)

def attend(queries, keys, values, query_ids, key_ids):
    rows = queries.shape[0]
    query_heads = queries.astype(jnp.float32).reshape(rows, HEADS, HD)
    key_heads = keys.astype(jnp.float32).reshape(keys.shape[0], HEADS, HD)
    value_heads = values.astype(jnp.float32).reshape(values.shape[0], HEADS, HD)
    logits = jnp.einsum('qhd,khd->hqk', query_heads, key_heads, precision=lax.Precision.HIGHEST) * (1.0 / math.sqrt(HD))
    same = query_ids[:, None] == key_ids[None, :]
    logits = jnp.where(same[None], logits, -1e+30)
    peak = lax.optimization_barrier(jnp.max(logits, axis=2, keepdims=True))
    weights = jnp.exp(logits - peak)
    probs = (weights / lax.optimization_barrier(jnp.sum(weights, axis=2, keepdims=True))).astype(jnp.bfloat16)
    result = jnp.einsum('hqk,khd->qhd', probs.astype(jnp.float32), value_heads, precision=lax.Precision.HIGHEST)
    return result.astype(jnp.bfloat16).reshape(rows, HEADS * HD)

def attend_near(queries, keys, values, token_ids, block_rows):
    keys_pad = jnp.pad(keys, ((block_rows, block_rows), (0, 0)))
    values_pad = jnp.pad(values, ((block_rows, block_rows), (0, 0)))
    ids_pad = jnp.pad(token_ids, (block_rows, block_rows), constant_values=-1)
    holder_total = queries.shape[0] // block_rows

    def one_holder(index):
        start = (index * block_rows).astype(jnp.int32)
        own_queries = lax.dynamic_slice_in_dim(queries, start, block_rows, 0)
        near_keys = lax.dynamic_slice_in_dim(keys_pad, start, 3 * block_rows, 0)
        near_values = lax.dynamic_slice_in_dim(values_pad, start, 3 * block_rows, 0)
        own_ids = lax.dynamic_slice_in_dim(token_ids, start, block_rows, 0)
        near_ids = lax.dynamic_slice_in_dim(ids_pad, start, 3 * block_rows, 0)
        return attend(own_queries, near_keys, near_values, own_ids, near_ids)
    outputs = lax.map(one_holder, jnp.arange(holder_total, dtype=jnp.int32))
    return outputs.reshape(queries.shape[0], HW)

def reference(canvas, conv_weight, conv_bias, score_weight, tile_tokens, tile_cell, tile_count, holder_order, tile_image, ln_gain, qkv_weight):
    padded = jnp.pad(canvas, ((1, 1), (1, 1), (0, 0)))
    bands = []
    for group in range(N_GRP):
        band = padded[group * CH:group * CH + CH + 2]
        bands.append(conv_scores(band, conv_weight, conv_bias, score_weight, CH, CW * N_DEV).reshape(CH, CW * N_DEV))
    score_map = jnp.concatenate(bands, 0)
    outputs = []
    for group in range(N_GRP):
        counts = tile_count[group]
        order = holder_order[group]
        prefix = jnp.cumsum(counts) - counts
        place = jnp.zeros((N_DEV,), jnp.int32).at[order].set(jnp.arange(N_DEV, dtype=jnp.int32))
        position = jnp.arange(MT, dtype=jnp.int32)[None, :] * N_DEV + place[:, None]
        source = lax.optimization_barrier(jnp.sum((prefix[None, None, :] <= position[:, :, None]).astype(jnp.int32), axis=2)) - 1
        slot_index = position - prefix[source]
        flat = ((group * N_DEV + source) * SLOTS + slot_index).astype(jnp.int32)
        tokens = tile_tokens[flat.reshape(-1)].reshape(N_DEV * MT * TT, D)
        cells = tile_cell[group][(source * SLOTS + slot_index).astype(jnp.int32)]
        score_rows = (group * CH + cells // CW).astype(jnp.int32)
        score_cols = (source * CW + cells % CW).astype(jnp.int32)
        rounded = lax.optimization_barrier(score_map[score_rows, score_cols].astype(jnp.bfloat16))
        sharpness = 0.5 + jax.nn.softplus(rounded.astype(jnp.float32))
        sharpness = jnp.repeat(sharpness.reshape(-1), TT)
        normed = layer_norm(tokens, ln_gain)
        mixed = jnp.dot(normed, qkv_weight, preferred_element_type=jnp.float32)
        queries = mixed[:, :HW].astype(jnp.bfloat16)
        keys = (mixed[:, HW:2 * HW] * sharpness[:, None]).astype(jnp.bfloat16)
        values = mixed[:, 2 * HW:].astype(jnp.bfloat16)
        token_ids = jnp.repeat(tile_image[group], TT).astype(jnp.int32)
        outputs.append(attend_near(queries, keys, values, token_ids, MT * TT))
    return (score_map, jnp.concatenate(outputs, 0))
```

```python
import math

import jax
import jax.numpy as jnp
from jax import lax
from jax.sharding import Mesh
from jax.sharding import PartitionSpec as P

HD = 128
HEADS = 13
MT = 8
PART = (HEADS + 1) // 2
ROW_PAD = 16


def line_exchange(last, initial, axis):
    size = lax.axis_size(axis)
    up = [(i, i + 1) for i in range(size - 1)]
    down = [(j, i) for i, j in up]
    return lax.ppermute(last, axis, up), lax.ppermute(initial, axis, down)


def dev_exchange(last, initial, axes):
    size = lax.axis_size(axes)
    up = [(i, i + 1) for i in range(size - 1)]
    down = [(j, i) for i, j in up]
    return lax.ppermute(last, axes, up), lax.ppermute(initial, axes, down)


def with_halo(value, axes, dim):
    length = value.shape[dim]
    before, after = dev_exchange(
        lax.slice_in_dim(value, length - 1, length, axis=dim),
        lax.slice_in_dim(value, 0, 1, axis=dim),
        axes,
    )
    return jnp.concatenate([before, value, after], axis=dim)


def swap_core(value):
    return lax.ppermute(value, "core", [(0, 1), (1, 0)])


def layer_norm(rows, gain):
    values = rows.astype(jnp.float32)
    center = jnp.mean(values, axis=1, keepdims=True)
    spread = jnp.mean(jnp.square(values - center), axis=1, keepdims=True)
    return ((values - center) * lax.rsqrt(spread + 1e-06) * gain).astype(jnp.bfloat16)


def conv_scores(padded, conv_weight, conv_bias, score_weight, height, breadth):
    channels = padded.shape[2]
    summed = jnp.zeros((height * breadth, conv_weight.shape[1]), jnp.float32)
    for row_off in range(3):
        for col_off in range(3):
            window = padded[row_off : row_off + height, col_off : col_off + breadth].reshape(
                height * breadth, channels
            )
            offset = (row_off * 3 + col_off) * channels
            summed = summed + jnp.dot(
                window, conv_weight[offset : offset + channels], preferred_element_type=jnp.float32
            )
    hidden = jax.nn.gelu(summed + conv_bias)
    return jnp.dot(hidden, score_weight, precision=lax.Precision.HIGHEST)


def attend(queries, keys, values, query_ids, key_ids):
    logits = jnp.einsum("bqhd,bkhd->bhqk", queries, keys, preferred_element_type=jnp.float32) * (
        1.0 / math.sqrt(HD)
    )
    same = query_ids[:, :, None] == key_ids[:, None, :]
    logits = jnp.where(same[:, None], logits, -1e30)
    peak = jnp.max(logits, axis=3, keepdims=True)
    weights = jnp.exp(logits - peak)
    probs = (weights / jnp.sum(weights, axis=3, keepdims=True)).astype(jnp.bfloat16)
    result = jnp.einsum("bhqk,bkhd->bqhd", probs, values, preferred_element_type=jnp.float32)
    return result.astype(jnp.bfloat16)


def core_heads(weight, core):
    rows = weight.shape[0]
    split = weight.reshape(rows, 3, HEADS, HD)
    low = split[:, :, :PART].reshape(rows, 3 * PART * HD)
    high = split[:, :, HEADS - PART :].reshape(rows, 3 * PART * HD)
    mine = jnp.where(core == 0, low, high)
    other = jnp.where(core == 0, high, low)
    return mine, other


def shards(
    canvas,
    conv_weight,
    conv_bias,
    score_weight,
    tile_tokens,
    tile_cell,
    tile_count,
    holder_order,
    tile_image,
    ln_gain,
    qkv_weight,
):
    dev = ("chip", "core")
    core = lax.axis_index("core")
    chip = lax.axis_index("chip")
    holders = lax.axis_size(dev)
    own_index = chip * 2 + core
    slot_count, tile_len, model_width = tile_tokens.shape
    rows_here = qkv_weight.shape[0]

    mine, other = core_heads(qkv_weight, core)
    theirs = swap_core(other)
    first = jnp.where(core == 0, mine, theirs)
    second = jnp.where(core == 0, theirs, mine)
    chip_rows = 2 * rows_here
    padded_rows = -(-chip_rows // ROW_PAD) * ROW_PAD
    fill = jnp.zeros((padded_rows - chip_rows, first.shape[1]), first.dtype)
    block = jnp.concatenate([first, second, fill], axis=0)
    weights = lax.all_gather(block, ("grp", "chip"), axis=0, tiled=True)

    per_peer = max(1, slot_count // holders)
    counts = tile_count[0]
    order = holder_order[0]
    slot_range = jnp.arange(slot_count, dtype=jnp.int32)
    round_range = jnp.arange(per_peer, dtype=jnp.int32)
    holder_range = jnp.arange(holders, dtype=jnp.int32)
    prefix = jnp.sum(
        jnp.where(holder_range[None, :] < holder_range[:, None], counts[None, :], 0), axis=1
    )
    is_me = holder_range == own_index
    position = jnp.sum(jnp.where(is_me, prefix, 0)) + slot_range
    is_live = slot_range < jnp.sum(jnp.where(is_me, counts, 0))
    hit = (position % holders)[:, None] == holder_range[None, :]
    target = jnp.sum(jnp.where(hit, order[None, :], 0), axis=1)
    same_holder = target[None, None, :] == holder_range[:, None, None]
    same_round = (slot_range // holders)[None, None, :] == round_range[None, :, None]
    send_mask = (same_holder & same_round & is_live[None, None, :]).astype(jnp.bfloat16)
    send_tiles = jnp.einsum(
        "kcs,std->kctd", send_mask, tile_tokens, preferred_element_type=jnp.float32
    ).astype(jnp.bfloat16)
    send_tiles, canvas = lax.optimization_barrier((send_tiles, canvas))
    recv_tiles = lax.all_to_all(send_tiles, dev, split_axis=0, concat_axis=0, tiled=True)

    height, breadth = canvas.shape[0], canvas.shape[1]
    padded = with_halo(with_halo(canvas, "grp", 0), dev, 1)
    score_flat = conv_scores(padded, conv_weight, conv_bias, score_weight, height, breadth)
    score_map = score_flat.reshape(height, breadth)
    tile_score = jnp.take(score_flat, tile_cell[0]).astype(jnp.bfloat16)
    send_score = jnp.einsum(
        "kcs,s->kc", send_mask, tile_score, preferred_element_type=jnp.float32
    ).astype(jnp.bfloat16)
    recv_score = lax.all_to_all(send_score, dev, split_axis=0, concat_axis=0, tiled=True)

    place = jnp.sum(jnp.where(order == own_index, holder_range, 0))
    wanted = jnp.arange(MT, dtype=jnp.int32) * holders + place
    from_source = (prefix[None, :] <= wanted[:, None]) & (
        wanted[:, None] < (prefix + counts)[None, :]
    )
    round_of = (wanted[:, None] - prefix[None, :]) // holders
    take_mask = (
        from_source[:, :, None] & (round_of[:, :, None] == round_range[None, None, :])
    ).astype(jnp.bfloat16)
    held_score = jnp.einsum(
        "mjc,jc->m", take_mask, recv_score, preferred_element_type=jnp.float32
    ).astype(jnp.bfloat16)
    held = jnp.einsum(
        "mjc,jctd->mtd", take_mask, recv_tiles, preferred_element_type=jnp.float32
    ).astype(jnp.bfloat16)
    held_rows = MT * tile_len
    normed = layer_norm(held.reshape(held_rows, model_width), ln_gain)

    def both(value):
        far = swap_core(value)
        return jnp.concatenate(
            [jnp.where(core == 0, value, far), jnp.where(core == 0, far, value)], axis=0
        )

    chip_score = both(held_score)
    sharpness = jnp.repeat(0.5 + jax.nn.softplus(chip_score.astype(jnp.float32)), tile_len)
    chip_normed = both(normed)
    blocks = model_width // chip_rows
    chip_normed = jnp.pad(
        chip_normed.reshape(2 * held_rows, blocks, chip_rows),
        ((0, 0), (0, 0), (0, padded_rows - chip_rows)),
    ).reshape(2 * held_rows, blocks * padded_rows)

    mixed = jnp.dot(chip_normed, weights, preferred_element_type=jnp.float32)
    part = PART * HD
    queries = mixed[:, :part].astype(jnp.bfloat16)
    keys = (mixed[:, part : 2 * part] * sharpness[:, None]).astype(jnp.bfloat16)
    values = mixed[:, 2 * part :].astype(jnp.bfloat16)
    key_value = jnp.concatenate([keys, values], axis=1)
    before, after = line_exchange(key_value[held_rows:], key_value[:held_rows], "chip")
    near = jnp.concatenate([before, key_value, after], axis=0)
    near = jnp.stack([near[: 3 * held_rows], near[held_rows:]], axis=0)
    near = near.reshape(2, 3 * held_rows, 2, PART, HD)

    all_ids = tile_image[0]
    tile_total = all_ids.shape[0]
    chip_tiles = 2 * MT
    ids_pad = jnp.pad(all_ids, (MT, MT), constant_values=-1)
    near_ids = lax.dynamic_slice_in_dim(ids_pad, chip * chip_tiles, chip_tiles + 2 * MT)
    key_ids = jnp.stack([near_ids[: 3 * MT], near_ids[MT:]], axis=0)
    key_ids = jnp.repeat(key_ids, tile_len, axis=1)
    own_ids = jnp.repeat(near_ids[MT:-MT].reshape(2, MT), tile_len, axis=1)
    result = attend(
        queries.reshape(2, held_rows, PART, HD), near[:, :, 0], near[:, :, 1], own_ids, key_ids
    ).reshape(2, held_rows, part)
    mine_out = jnp.where(core == 0, result[0], result[1])
    far_out = swap_core(jnp.where(core == 0, result[1], result[0]))
    low = jnp.where(core == 0, mine_out, far_out)
    high = jnp.where(core == 0, far_out, mine_out)
    skip = (2 * PART - HEADS) * HD
    attended = jnp.concatenate([low, high[:, skip:]], axis=1)
    return (score_map, attended)


def solution(mesh):
    groups, devs = mesh.devices.shape
    fine = Mesh(mesh.devices.reshape(groups, devs // 2, 2), ("grp", "chip", "core"))
    dev = ("chip", "core")
    every = ("grp", "chip", "core")
    placed = (
        P("grp", dev, None),
        P(),
        P(),
        P(),
        P(every, None, None),
        P("grp", dev),
        P("grp", None),
        P("grp", None),
        P("grp", None),
        P(),
        P(every, None),
    )
    return jax.shard_map(
        shards,
        mesh=fine,
        in_specs=placed,
        out_specs=(P("grp", dev), P(every, None)),
        check_vma=False,
    )
```

```python
import math

import jax
import jax.numpy as jnp
from jax import lax
from jax.sharding import Mesh
from jax.sharding import PartitionSpec as P

HD = 128
HEADS = 13
MT = 8
PART = (HEADS + 1) // 2
ROW_PAD = 16


def line_exchange(last, initial, axis):
    size = lax.axis_size(axis)
    up = [(i, i + 1) for i in range(size - 1)]
    down = [(j, i) for i, j in up]
    return lax.ppermute(last, axis, up), lax.ppermute(initial, axis, down)


def dev_exchange(last, initial, axes):
    size = lax.axis_size(axes)
    up = [(i, i + 1) for i in range(size - 1)]
    down = [(j, i) for i, j in up]
    return lax.ppermute(last, axes, up), lax.ppermute(initial, axes, down)


def with_halo(value, axes, dim):
    length = value.shape[dim]
    before, after = dev_exchange(
        lax.slice_in_dim(value, length - 1, length, axis=dim),
        lax.slice_in_dim(value, 0, 1, axis=dim),
        axes,
    )
    return jnp.concatenate([before, value, after], axis=dim)


def swap_core(value):
    return lax.ppermute(value, "core", [(0, 1), (1, 0)])


def layer_norm(rows, gain):
    values = rows.astype(jnp.float32)
    center = jnp.mean(values, axis=1, keepdims=True)
    spread = jnp.mean(jnp.square(values - center), axis=1, keepdims=True)
    return ((values - center) * lax.rsqrt(spread + 1e-06) * gain).astype(jnp.bfloat16)


def conv_scores(padded, conv_weight, conv_bias, score_weight, height, breadth):
    channels = padded.shape[2]
    summed = jnp.zeros((height * breadth, conv_weight.shape[1]), jnp.float32)
    for row_off in range(3):
        for col_off in range(3):
            window = padded[row_off : row_off + height, col_off : col_off + breadth].reshape(
                height * breadth, channels
            )
            offset = (row_off * 3 + col_off) * channels
            summed = summed + jnp.dot(
                window, conv_weight[offset : offset + channels], preferred_element_type=jnp.float32
            )
    hidden = jax.nn.gelu(summed + conv_bias)
    return jnp.dot(hidden, score_weight, precision=lax.Precision.HIGHEST)


def attend(queries, keys, values, query_ids, key_ids):
    logits = jnp.einsum("bqhd,bkhd->bhqk", queries, keys, preferred_element_type=jnp.float32) * (
        1.0 / math.sqrt(HD)
    )
    same = query_ids[:, :, None] == key_ids[:, None, :]
    logits = jnp.where(same[:, None], logits, -1e30)
    peak = jnp.max(logits, axis=3, keepdims=True)
    weights = jnp.exp(logits - peak)
    probs = (weights / jnp.sum(weights, axis=3, keepdims=True)).astype(jnp.bfloat16)
    result = jnp.einsum("bhqk,bkhd->bqhd", probs, values, preferred_element_type=jnp.float32)
    return result.astype(jnp.bfloat16)


def core_heads(weight, core):
    rows = weight.shape[0]
    split = weight.reshape(rows, 3, HEADS, HD)
    low = split[:, :, :PART].reshape(rows, 3 * PART * HD)
    high = split[:, :, HEADS - PART :].reshape(rows, 3 * PART * HD)
    mine = jnp.where(core == 0, low, high)
    other = jnp.where(core == 0, high, low)
    return mine, other


def shards_by_core(
    canvas,
    conv_weight,
    conv_bias,
    score_weight,
    tile_tokens,
    tile_cell,
    tile_count,
    holder_order,
    tile_image,
    ln_gain,
    qkv_weight,
):
    dev = ("chip", "core")
    core = lax.axis_index("core")
    chip = lax.axis_index("chip")
    holders = lax.axis_size(dev)
    own_index = chip * 2 + core
    slot_count, tile_len, model_width = tile_tokens.shape
    rows_here = qkv_weight.shape[0]

    mine, other = core_heads(qkv_weight, core)
    theirs = swap_core(other)
    first = jnp.where(core == 0, mine, theirs)
    second = jnp.where(core == 0, theirs, mine)
    chip_rows = 2 * rows_here
    padded_rows = -(-chip_rows // ROW_PAD) * ROW_PAD
    fill = jnp.zeros((padded_rows - chip_rows, first.shape[1]), first.dtype)
    block = jnp.concatenate([first, second, fill], axis=0)
    weights = lax.all_gather(block, ("grp", "chip"), axis=0, tiled=True)

    per_peer = max(1, slot_count // holders)
    counts = tile_count[0]
    order = holder_order[0]
    slot_range = jnp.arange(slot_count, dtype=jnp.int32)
    round_range = jnp.arange(per_peer, dtype=jnp.int32)
    holder_range = jnp.arange(holders, dtype=jnp.int32)
    prefix = jnp.sum(
        jnp.where(holder_range[None, :] < holder_range[:, None], counts[None, :], 0), axis=1
    )
    is_me = holder_range == own_index
    position = jnp.sum(jnp.where(is_me, prefix, 0)) + slot_range
    is_live = slot_range < jnp.sum(jnp.where(is_me, counts, 0))
    hit = (position % holders)[:, None] == holder_range[None, :]
    target = jnp.sum(jnp.where(hit, order[None, :], 0), axis=1)
    same_holder = target[None, None, :] == holder_range[:, None, None]
    same_round = (slot_range // holders)[None, None, :] == round_range[None, :, None]
    send_mask = (same_holder & same_round & is_live[None, None, :]).astype(jnp.bfloat16)
    send_tiles = jnp.einsum(
        "kcs,std->kctd", send_mask, tile_tokens, preferred_element_type=jnp.float32
    ).astype(jnp.bfloat16)
    send_tiles, canvas = lax.optimization_barrier((send_tiles, canvas))
    recv_tiles = lax.all_to_all(send_tiles, dev, split_axis=0, concat_axis=0, tiled=True)

    height, breadth = canvas.shape[0], canvas.shape[1]
    padded = with_halo(with_halo(canvas, "grp", 0), dev, 1)
    score_flat = conv_scores(padded, conv_weight, conv_bias, score_weight, height, breadth)
    score_map = score_flat.reshape(height, breadth)
    tile_score = jnp.take(score_flat, tile_cell[0]).astype(jnp.bfloat16)
    send_score = jnp.einsum(
        "kcs,s->kc", send_mask, tile_score, preferred_element_type=jnp.float32
    ).astype(jnp.bfloat16)
    recv_score = lax.all_to_all(send_score, dev, split_axis=0, concat_axis=0, tiled=True)

    place = jnp.sum(jnp.where(order == own_index, holder_range, 0))
    wanted = jnp.arange(MT, dtype=jnp.int32) * holders + place
    from_source = (prefix[None, :] <= wanted[:, None]) & (
        wanted[:, None] < (prefix + counts)[None, :]
    )
    round_of = (wanted[:, None] - prefix[None, :]) // holders
    take_mask = (
        from_source[:, :, None] & (round_of[:, :, None] == round_range[None, None, :])
    ).astype(jnp.bfloat16)
    held_score = jnp.einsum(
        "mjc,jc->m", take_mask, recv_score, preferred_element_type=jnp.float32
    ).astype(jnp.bfloat16)
    held = jnp.einsum(
        "mjc,jctd->mtd", take_mask, recv_tiles, preferred_element_type=jnp.float32
    ).astype(jnp.bfloat16)
    held_rows = MT * tile_len
    normed = layer_norm(held.reshape(held_rows, model_width), ln_gain)

    def both(value):
        far = swap_core(value)
        return jnp.concatenate(
            [jnp.where(core == 0, value, far), jnp.where(core == 0, far, value)], axis=0
        )

    chip_score = both(held_score)
    sharpness = jnp.repeat(0.5 + jax.nn.softplus(chip_score.astype(jnp.float32)), tile_len)
    chip_normed = both(normed)
    blocks = model_width // chip_rows
    chip_normed = jnp.pad(
        chip_normed.reshape(2 * held_rows, blocks, chip_rows),
        ((0, 0), (0, 0), (0, padded_rows - chip_rows)),
    ).reshape(2 * held_rows, blocks * padded_rows)

    mixed = jnp.dot(chip_normed, weights, preferred_element_type=jnp.float32)
    part = PART * HD
    queries = mixed[:, :part].astype(jnp.bfloat16)
    keys = (mixed[:, part : 2 * part] * sharpness[:, None]).astype(jnp.bfloat16)
    values = mixed[:, 2 * part :].astype(jnp.bfloat16)
    key_value = jnp.concatenate([keys, values], axis=1)
    before, after = line_exchange(key_value[held_rows:], key_value[:held_rows], "chip")
    near = jnp.concatenate([before, key_value, after], axis=0)
    near = jnp.stack([near[: 3 * held_rows], near[held_rows:]], axis=0)
    near = near.reshape(2, 3 * held_rows, 2, PART, HD)

    all_ids = tile_image[0]
    tile_total = all_ids.shape[0]
    chip_tiles = 2 * MT
    ids_pad = jnp.pad(all_ids, (MT, MT), constant_values=-1)
    near_ids = lax.dynamic_slice_in_dim(ids_pad, chip * chip_tiles, chip_tiles + 2 * MT)
    key_ids = jnp.stack([near_ids[: 3 * MT], near_ids[MT:]], axis=0)
    key_ids = jnp.repeat(key_ids, tile_len, axis=1)
    own_ids = jnp.repeat(near_ids[MT:-MT].reshape(2, MT), tile_len, axis=1)
    result = attend(
        queries.reshape(2, held_rows, PART, HD), near[:, :, 0], near[:, :, 1], own_ids, key_ids
    ).reshape(2, held_rows, part)
    mine_out = jnp.where(core == 0, result[0], result[1])
    far_out = swap_core(jnp.where(core == 0, result[1], result[0]))
    low = jnp.where(core == 0, mine_out, far_out)
    high = jnp.where(core == 0, far_out, mine_out)
    skip = (2 * PART - HEADS) * HD
    attended = jnp.concatenate([low, high[:, skip:]], axis=1)
    return (score_map, attended)


def prefix_of(counts, holder_range):
    earlier = holder_range[None, :] < holder_range[:, None]
    return jnp.sum(jnp.where(earlier, counts[None, :], 0), axis=1)


def hop_pairs(hop, chips):
    return [(hop, hop + 1), (chips - 1 - hop, chips - 2 - hop)]


def merge_line(chunks, chips):
    total = list(chunks)
    got = [None] * len(chunks)
    waves = []
    for step in range(len(chunks) + chips - 2):
        arrived = []
        for hop in reversed(range(chips - 1)):
            at = step - hop
            if not 0 <= at < len(chunks):
                continue
            load = chunks[at] if hop == 0 else chunks[at] + got[at]
            if len(waves) >= 2:
                load, waves[-2] = lax.optimization_barrier((load, waves[-2]))
            fresh = lax.ppermute(load, "chip", hop_pairs(hop, chips))
            arrived.append((at, fresh))
        for at, fresh in arrived:
            got[at] = fresh
            total[at] = total[at] + fresh
        waves.append([fresh for _, fresh in arrived])
    return total


def shards_by_head(
    canvas,
    conv_weight,
    conv_bias,
    score_weight,
    tile_tokens,
    tile_cell,
    tile_count,
    holder_order,
    tile_image,
    ln_gain,
    qkv_weight,
):
    dev = ("chip", "core")
    core = lax.axis_index("core")
    chips = lax.axis_size("chip")
    holders = lax.axis_size(dev)
    groups = lax.axis_size("grp")
    group = lax.axis_index("grp")
    own_index = lax.axis_index("chip") * 2 + core
    slot_count, tile_len, model_width = tile_tokens.shape
    rows_here = qkv_weight.shape[0]
    each = -(-HEADS // holders)
    wide = each * HD
    first_head = [min(each * d, HEADS - each) for d in range(holders)]

    counts = tile_count[0]
    order = holder_order[0]
    total = holders * MT
    slot_range = jnp.arange(slot_count, dtype=jnp.int32)
    holder_range = jnp.arange(holders, dtype=jnp.int32)
    prefix = prefix_of(counts, holder_range)
    is_me = holder_range == own_index
    my_start = jnp.sum(jnp.where(is_me, prefix, 0))
    my_count = jnp.sum(jnp.where(is_me, counts, 0))
    place = jnp.sum(
        jnp.where(order[None, :] == holder_range[:, None], holder_range[None, :], 0), axis=1
    )
    position = (
        jnp.arange(MT, dtype=jnp.int32)[None, :] * holders + place[:, None]
    ).reshape(total)
    source_slot = position - my_start
    source = (source_slot[:, None] == slot_range[None, :]) & (slot_range < my_count)[None, :]
    source = source.astype(jnp.bfloat16)
    half = total // 2
    mine_mask = jnp.where(core == 0, source[:half], source[half:])
    other_mask = jnp.where(core == 0, source[half:], source[:half])

    def pick(mask):
        return jnp.einsum(
            "ps,std->ptd", mask, tile_tokens, preferred_element_type=jnp.float32
        ).astype(jnp.bfloat16)

    n_chunks = 8
    per_chunk = half // n_chunks
    given = pick(other_mask).reshape(half * tile_len, model_width)
    kept = pick(mine_mask).reshape(half * tile_len, model_width)
    chip_half = kept + swap_core(given)
    chunk_rows = per_chunk * tile_len
    chunks = [chip_half[i * chunk_rows : (i + 1) * chunk_rows] for i in range(n_chunks)]

    split = qkv_weight.reshape(rows_here, 3, HEADS, HD)
    send_weight = jnp.stack(
        [split[:, :, h : h + each].reshape(rows_here, 3 * wide) for h in first_head], axis=0
    )
    chunks[0], send_weight = lax.optimization_barrier((chunks[0], send_weight))
    block = lax.all_to_all(send_weight, dev, split_axis=0, concat_axis=0, tiled=True)
    block = block.reshape(holders * rows_here, 3 * wide)
    group_rows = holders * rows_here
    weights = jnp.zeros((groups * group_rows, 3 * wide), jnp.bfloat16)
    weights = lax.dynamic_update_slice_in_dim(weights, block, group * group_rows, 0)
    for shift in range(1, groups):
        far = lax.ppermute(block, "grp", [(i, (i + shift) % groups) for i in range(groups)])
        weights = lax.dynamic_update_slice_in_dim(
            weights, far, ((group - shift) % groups) * group_rows, 0
        )

    canvas, chunks[0] = lax.optimization_barrier((canvas, chunks[0]))
    height, breadth = canvas.shape[0], canvas.shape[1]
    padded = with_halo(with_halo(canvas, "grp", 0), dev, 1)
    score_flat = conv_scores(padded, conv_weight, conv_bias, score_weight, height, breadth)
    score_map = score_flat.reshape(height, breadth)
    tile_score = jnp.take(score_flat, tile_cell[0]).astype(jnp.bfloat16)
    own_scores = jnp.sum(source.astype(jnp.float32) * tile_score.astype(jnp.float32), axis=1)
    held_score = lax.psum(own_scores, dev)
    sharpness = jnp.repeat(0.5 + jax.nn.softplus(held_score), tile_len)

    merged = merge_line(chunks, chips)
    normed = [layer_norm(rows, ln_gain) for rows in merged]
    far = [swap_core(rows) for rows in normed]
    near_half, far_half = jnp.concatenate(normed, axis=0), jnp.concatenate(far, axis=0)
    near_mixed = jnp.dot(near_half, weights, preferred_element_type=jnp.float32)
    far_mixed = jnp.dot(far_half, weights, preferred_element_type=jnp.float32)
    mixed = jnp.concatenate(
        [jnp.where(core == 0, near_mixed, far_mixed), jnp.where(core == 0, far_mixed, near_mixed)],
        axis=0,
    )
    queries = mixed[:, :wide].astype(jnp.bfloat16)
    keys = (mixed[:, wide : 2 * wide] * sharpness[:, None]).astype(jnp.bfloat16)
    values = mixed[:, 2 * wide :].astype(jnp.bfloat16)

    held_rows = MT * tile_len
    token_ids = jnp.repeat(tile_image[0], tile_len)

    def banded(value, fill):
        edge = [(held_rows, held_rows)] + [(0, 0)] * (value.ndim - 1)
        blocks = jnp.pad(value, edge, constant_values=fill)
        blocks = blocks.reshape((holders + 2, held_rows) + value.shape[1:])
        return jnp.concatenate([blocks[:-2], blocks[1:-1], blocks[2:]], axis=1)

    key_ids = banded(token_ids, -1)
    own_ids = token_ids.reshape(holders, held_rows)
    outs = []
    for head in range(each):
        lanes = slice(head * HD, (head + 1) * HD)
        outs.append(
            attend(
                queries[:, lanes].reshape(holders, held_rows, 1, HD),
                banded(keys[:, lanes], 0)[:, :, None],
                banded(values[:, lanes], 0)[:, :, None],
                own_ids,
                key_ids,
            )[:, :, 0]
        )
    mine = jnp.concatenate(outs, axis=2)
    heads_in = lax.all_to_all(mine, dev, split_axis=0, concat_axis=0, tiled=True)
    parts, done = [], 0
    for d in range(holders):
        if done < HEADS:
            skip = done - first_head[d]
            parts.append(heads_in[d][:, skip * HD :])
            done = first_head[d] + each
    return (score_map, jnp.concatenate(parts, axis=1))


def solution(mesh):
    groups, devs = mesh.devices.shape
    fine = Mesh(mesh.devices.reshape(groups, devs // 2, 2), ("grp", "chip", "core"))
    dev = ("chip", "core")
    every = ("grp", "chip", "core")
    placed = (
        P("grp", dev, None),
        P(),
        P(),
        P(),
        P(every, None, None),
        P("grp", dev),
        P("grp", None),
        P("grp", None),
        P("grp", None),
        P(),
        P(every, None),
    )
    return jax.shard_map(
        shards_by_head if devs <= HEADS else shards_by_core,
        mesh=fine,
        in_specs=placed,
        out_specs=(P("grp", dev), P(every, None)),
        check_vma=False,
    )
```

```python
import functools
import math

import jax
import jax.numpy as jnp
from jax import lax
from jax.experimental import pallas as pl
from jax.experimental.pallas import tpu as pltpu
from jax.sharding import Mesh
from jax.sharding import PartitionSpec as P

HD = 128
HEADS = 13
MT = 8
PART = (HEADS + 1) // 2
ROW_PAD = 16


def line_exchange(last, initial, axis):
    size = lax.axis_size(axis)
    up = [(i, i + 1) for i in range(size - 1)]
    down = [(j, i) for i, j in up]
    return lax.ppermute(last, axis, up), lax.ppermute(initial, axis, down)


def dev_exchange(last, initial, axes):
    size = lax.axis_size(axes)
    up = [(i, i + 1) for i in range(size - 1)]
    down = [(j, i) for i, j in up]
    return lax.ppermute(last, axes, up), lax.ppermute(initial, axes, down)


def with_halo(value, axes, dim):
    length = value.shape[dim]
    before, after = dev_exchange(
        lax.slice_in_dim(value, length - 1, length, axis=dim),
        lax.slice_in_dim(value, 0, 1, axis=dim),
        axes,
    )
    return jnp.concatenate([before, value, after], axis=dim)


def swap_core(value):
    return lax.ppermute(value, "core", [(0, 1), (1, 0)])


def layer_norm(rows, gain):
    values = rows.astype(jnp.float32)
    center = jnp.mean(values, axis=1, keepdims=True)
    spread = jnp.mean(jnp.square(values - center), axis=1, keepdims=True)
    return ((values - center) * lax.rsqrt(spread + 1e-06) * gain).astype(jnp.bfloat16)


def conv_scores(padded, conv_weight, conv_bias, score_weight, height, breadth):
    channels = padded.shape[2]
    summed = jnp.zeros((height * breadth, conv_weight.shape[1]), jnp.float32)
    for row_off in range(3):
        for col_off in range(3):
            window = padded[row_off : row_off + height, col_off : col_off + breadth].reshape(
                height * breadth, channels
            )
            offset = (row_off * 3 + col_off) * channels
            summed = summed + jnp.dot(
                window, conv_weight[offset : offset + channels], preferred_element_type=jnp.float32
            )
    hidden = jax.nn.gelu(summed + conv_bias)
    return jnp.dot(hidden, score_weight, precision=lax.Precision.HIGHEST)


def attend(queries, keys, values, query_ids, key_ids):
    logits = jnp.einsum("bqhd,bkhd->bhqk", queries, keys, preferred_element_type=jnp.float32) * (
        1.0 / math.sqrt(HD)
    )
    same = query_ids[:, :, None] == key_ids[:, None, :]
    logits = jnp.where(same[:, None], logits, -1e30)
    peak = jnp.max(logits, axis=3, keepdims=True)
    weights = jnp.exp(logits - peak)
    probs = (weights / jnp.sum(weights, axis=3, keepdims=True)).astype(jnp.bfloat16)
    result = jnp.einsum("bhqk,bkhd->bqhd", probs, values, preferred_element_type=jnp.float32)
    return result.astype(jnp.bfloat16)


def core_heads(weight, core):
    rows = weight.shape[0]
    split = weight.reshape(rows, 3, HEADS, HD)
    low = split[:, :, :PART].reshape(rows, 3 * PART * HD)
    high = split[:, :, HEADS - PART :].reshape(rows, 3 * PART * HD)
    mine = jnp.where(core == 0, low, high)
    other = jnp.where(core == 0, high, low)
    return mine, other


def shards_by_core(
    canvas,
    conv_weight,
    conv_bias,
    score_weight,
    tile_tokens,
    tile_cell,
    tile_count,
    holder_order,
    tile_image,
    ln_gain,
    qkv_weight,
):
    dev = ("chip", "core")
    core = lax.axis_index("core")
    chip = lax.axis_index("chip")
    holders = lax.axis_size(dev)
    own_index = chip * 2 + core
    slot_count, tile_len, model_width = tile_tokens.shape
    rows_here = qkv_weight.shape[0]

    mine, other = core_heads(qkv_weight, core)
    theirs = swap_core(other)
    first = jnp.where(core == 0, mine, theirs)
    second = jnp.where(core == 0, theirs, mine)
    chip_rows = 2 * rows_here
    padded_rows = -(-chip_rows // ROW_PAD) * ROW_PAD
    fill = jnp.zeros((padded_rows - chip_rows, first.shape[1]), first.dtype)
    block = jnp.concatenate([first, second, fill], axis=0)
    weights = lax.all_gather(block, ("grp", "chip"), axis=0, tiled=True)

    per_peer = max(1, slot_count // holders)
    counts = tile_count[0]
    order = holder_order[0]
    slot_range = jnp.arange(slot_count, dtype=jnp.int32)
    round_range = jnp.arange(per_peer, dtype=jnp.int32)
    holder_range = jnp.arange(holders, dtype=jnp.int32)
    prefix = jnp.sum(
        jnp.where(holder_range[None, :] < holder_range[:, None], counts[None, :], 0), axis=1
    )
    is_me = holder_range == own_index
    position = jnp.sum(jnp.where(is_me, prefix, 0)) + slot_range
    is_live = slot_range < jnp.sum(jnp.where(is_me, counts, 0))
    hit = (position % holders)[:, None] == holder_range[None, :]
    target = jnp.sum(jnp.where(hit, order[None, :], 0), axis=1)
    same_holder = target[None, None, :] == holder_range[:, None, None]
    same_round = (slot_range // holders)[None, None, :] == round_range[None, :, None]
    send_mask = (same_holder & same_round & is_live[None, None, :]).astype(jnp.bfloat16)
    send_tiles = jnp.einsum(
        "kcs,std->kctd", send_mask, tile_tokens, preferred_element_type=jnp.float32
    ).astype(jnp.bfloat16)
    send_tiles, canvas = lax.optimization_barrier((send_tiles, canvas))
    recv_tiles = lax.all_to_all(send_tiles, dev, split_axis=0, concat_axis=0, tiled=True)

    height, breadth = canvas.shape[0], canvas.shape[1]
    padded = with_halo(with_halo(canvas, "grp", 0), dev, 1)
    score_flat = conv_scores(padded, conv_weight, conv_bias, score_weight, height, breadth)
    score_map = score_flat.reshape(height, breadth)
    tile_score = jnp.take(score_flat, tile_cell[0]).astype(jnp.bfloat16)
    send_score = jnp.einsum(
        "kcs,s->kc", send_mask, tile_score, preferred_element_type=jnp.float32
    ).astype(jnp.bfloat16)
    recv_score = lax.all_to_all(send_score, dev, split_axis=0, concat_axis=0, tiled=True)

    place = jnp.sum(jnp.where(order == own_index, holder_range, 0))
    wanted = jnp.arange(MT, dtype=jnp.int32) * holders + place
    from_source = (prefix[None, :] <= wanted[:, None]) & (
        wanted[:, None] < (prefix + counts)[None, :]
    )
    round_of = (wanted[:, None] - prefix[None, :]) // holders
    take_mask = (
        from_source[:, :, None] & (round_of[:, :, None] == round_range[None, None, :])
    ).astype(jnp.bfloat16)
    held_score = jnp.einsum(
        "mjc,jc->m", take_mask, recv_score, preferred_element_type=jnp.float32
    ).astype(jnp.bfloat16)
    held = jnp.einsum(
        "mjc,jctd->mtd", take_mask, recv_tiles, preferred_element_type=jnp.float32
    ).astype(jnp.bfloat16)
    held_rows = MT * tile_len
    normed = layer_norm(held.reshape(held_rows, model_width), ln_gain)

    def both(value):
        far = swap_core(value)
        return jnp.concatenate(
            [jnp.where(core == 0, value, far), jnp.where(core == 0, far, value)], axis=0
        )

    chip_score = both(held_score)
    sharpness = jnp.repeat(0.5 + jax.nn.softplus(chip_score.astype(jnp.float32)), tile_len)
    chip_normed = both(normed)
    blocks = model_width // chip_rows
    chip_normed = jnp.pad(
        chip_normed.reshape(2 * held_rows, blocks, chip_rows),
        ((0, 0), (0, 0), (0, padded_rows - chip_rows)),
    ).reshape(2 * held_rows, blocks * padded_rows)

    mixed = jnp.dot(chip_normed, weights, preferred_element_type=jnp.float32)
    part = PART * HD
    queries = mixed[:, :part].astype(jnp.bfloat16)
    keys = (mixed[:, part : 2 * part] * sharpness[:, None]).astype(jnp.bfloat16)
    values = mixed[:, 2 * part :].astype(jnp.bfloat16)
    key_value = jnp.concatenate([keys, values], axis=1)
    before, after = line_exchange(key_value[held_rows:], key_value[:held_rows], "chip")
    near = jnp.concatenate([before, key_value, after], axis=0)
    near = jnp.stack([near[: 3 * held_rows], near[held_rows:]], axis=0)
    near = near.reshape(2, 3 * held_rows, 2, PART, HD)

    all_ids = tile_image[0]
    tile_total = all_ids.shape[0]
    chip_tiles = 2 * MT
    ids_pad = jnp.pad(all_ids, (MT, MT), constant_values=-1)
    near_ids = lax.dynamic_slice_in_dim(ids_pad, chip * chip_tiles, chip_tiles + 2 * MT)
    key_ids = jnp.stack([near_ids[: 3 * MT], near_ids[MT:]], axis=0)
    key_ids = jnp.repeat(key_ids, tile_len, axis=1)
    own_ids = jnp.repeat(near_ids[MT:-MT].reshape(2, MT), tile_len, axis=1)
    result = attend(
        queries.reshape(2, held_rows, PART, HD), near[:, :, 0], near[:, :, 1], own_ids, key_ids
    ).reshape(2, held_rows, part)
    mine_out = jnp.where(core == 0, result[0], result[1])
    far_out = swap_core(jnp.where(core == 0, result[1], result[0]))
    low = jnp.where(core == 0, mine_out, far_out)
    high = jnp.where(core == 0, far_out, mine_out)
    skip = (2 * PART - HEADS) * HD
    attended = jnp.concatenate([low, high[:, skip:]], axis=1)
    return (score_map, attended)


def prefix_of(counts, holder_range):
    earlier = holder_range[None, :] < holder_range[:, None]
    return jnp.sum(jnp.where(earlier, counts[None, :], 0), axis=1)


def merge_kernel(chips, chunks, rows, own, weight, gain, mixed, *scratch):
    right_in, left_in, normed, tile, r_send, r_recv, l_send, l_recv, c_send, c_recv = scratch
    chip, core = lax.axis_index("chip"), lax.axis_index("core")
    half = chunks * rows
    last = chips - 1
    nxt, prv = lax.rem(chip + 1, chips), lax.rem(chip + chips - 1, chips)
    mesh_id = pl.DeviceIdType.MESH

    barrier = pltpu.get_barrier_semaphore()
    pl.semaphore_signal(barrier, inc=1, device_id={"core": 1 - core}, device_id_type=mesh_id)

    @pl.when(chip > 0)
    def _():
        pl.semaphore_signal(barrier, inc=1, device_id={"chip": prv}, device_id_type=mesh_id)

    @pl.when(chip < last)
    def _():
        pl.semaphore_signal(barrier, inc=1, device_id={"chip": nxt}, device_id_type=mesh_id)

    inner = (chip > 0) & (chip < last)

    @pl.when(inner)
    def _():
        pl.semaphore_wait(barrier, 3)

    @pl.when(jnp.logical_not(inner))
    def _():
        pl.semaphore_wait(barrier, 2)

    def span(c):
        return pl.ds(pl.multiple_of(c * rows, rows), rows)

    def to_right(c, source):
        return pltpu.make_async_remote_copy(
            source.at[span(c)], right_in.at[span(c)], r_send.at[c], r_recv.at[c],
            device_id={"chip": nxt}, device_id_type=mesh_id,
        )

    def to_left(c, source):
        return pltpu.make_async_remote_copy(
            source.at[span(c)], left_in.at[span(c)], l_send.at[c], l_recv.at[c],
            device_id={"chip": prv}, device_id_type=mesh_id,
        )

    def core_span(c, which):
        return pl.ds(pl.multiple_of(which * half + c * rows, rows), rows)

    def to_core(c):
        there = normed.at[core_span(c, core)]
        return pltpu.make_async_remote_copy(
            there, there, c_send.at[c], c_recv.at[c],
            device_id={"core": 1 - core}, device_id_type=mesh_id,
        )

    def each(body):
        def step(c, carry):
            body(c)
            return carry

        lax.fori_loop(0, chunks, step, 0)

    @pl.when(chip == 0)
    def _():
        each(lambda c: to_right(c, own).start())

    @pl.when(chip == last)
    def _():
        each(lambda c: to_left(c, own).start())

    def project(at):
        mixed[at] = jnp.dot(normed[at], weight[...], preferred_element_type=jnp.float32)

    def far(c):
        to_core(c).wait_recv()
        project(core_span(c, 1 - core))

    def step(c):
        at = span(c)

        @pl.when(chip > 0)
        def _():
            to_right(c, right_in).wait_recv()
            right_in[at] = right_in[at] + own[at]

            @pl.when(chip < last)
            def _():
                to_right(c, right_in).start()

        @pl.when(chip == 0)
        def _():
            right_in[at] = own[at]

        @pl.when(chip < last)
        def _():
            to_left(c, left_in).wait_recv()
            tile[...] = right_in[at] + left_in[at]

            @pl.when(chip > 0)
            def _():
                left_in[at] = left_in[at] + own[at]
                to_left(c, left_in).start()

        @pl.when(chip == last)
        def _():
            tile[...] = right_in[at]

        normed[core_span(c, core)] = layer_norm(tile[...], gain[...])
        to_core(c).start()
        project(core_span(c, core))

        @pl.when(c > 0)
        def _():
            far(c - 1)

    each(step)
    far(chunks - 1)
    each(lambda c: to_core(c).wait_send())

    @pl.when(chip < last)
    def _():
        each(lambda c: to_right(c, right_in).wait_send())

    @pl.when(chip > 0)
    def _():
        each(lambda c: to_left(c, left_in).wait_send())


def merge_project(own, weight, gain, chips, chunks):
    half, width = own.shape
    columns = weight.shape[1]
    rows = half // chunks
    vmem = pl.BlockSpec(memory_space=pltpu.VMEM)
    sems = pltpu.SemaphoreType.DMA((chunks,))
    return pl.pallas_call(
        functools.partial(merge_kernel, chips, chunks, rows),
        out_shape=jax.ShapeDtypeStruct((2 * half, columns), jnp.float32),
        in_specs=[vmem] * 3,
        out_specs=vmem,
        scratch_shapes=[
            pltpu.VMEM((half, width), jnp.bfloat16),
            pltpu.VMEM((half, width), jnp.bfloat16),
            pltpu.VMEM((2 * half, width), jnp.bfloat16),
            pltpu.VMEM((rows, width), jnp.bfloat16),
        ]
        + [sems] * 6,
        compiler_params=pltpu.CompilerParams(
            collective_id=0, has_side_effects=True, vmem_limit_bytes=50 * 2**20
        ),
        cost_estimate=pl.CostEstimate(
            flops=4 * half * width * columns, bytes_accessed=400 * 2**20, transcendentals=0
        ),
    )(own, weight, gain.reshape(1, width))


def sum_over_dev(value, chips):
    value = value + swap_core(value)
    shift = 1
    while shift < chips:
        value = value + lax.ppermute(value, "chip", [(i, i ^ shift) for i in range(chips)])
        shift *= 2
    return value


def shards_by_head(
    canvas,
    conv_weight,
    conv_bias,
    score_weight,
    tile_tokens,
    tile_cell,
    tile_count,
    holder_order,
    tile_image,
    ln_gain,
    qkv_weight,
):
    dev = ("chip", "core")
    core = lax.axis_index("core")
    chips = lax.axis_size("chip")
    holders = lax.axis_size(dev)
    groups = lax.axis_size("grp")
    group = lax.axis_index("grp")
    own_index = lax.axis_index("chip") * 2 + core
    slot_count, tile_len, model_width = tile_tokens.shape
    rows_here = qkv_weight.shape[0]
    each = -(-HEADS // holders)
    wide = each * HD
    first_head = [min(each * d, HEADS - each) for d in range(holders)]

    counts = tile_count[0]
    order = holder_order[0]
    total = holders * MT
    slot_range = jnp.arange(slot_count, dtype=jnp.int32)
    holder_range = jnp.arange(holders, dtype=jnp.int32)
    prefix = prefix_of(counts, holder_range)
    is_me = holder_range == own_index
    my_start = jnp.sum(jnp.where(is_me, prefix, 0))
    my_count = jnp.sum(jnp.where(is_me, counts, 0))
    place = jnp.sum(
        jnp.where(order[None, :] == holder_range[:, None], holder_range[None, :], 0), axis=1
    )
    position = (
        jnp.arange(MT, dtype=jnp.int32)[None, :] * holders + place[:, None]
    ).reshape(total)
    source_slot = position - my_start
    source = (source_slot[:, None] == slot_range[None, :]) & (slot_range < my_count)[None, :]
    source = source.astype(jnp.bfloat16)
    half = total // 2
    mine_mask = jnp.where(core == 0, source[:half], source[half:])
    other_mask = jnp.where(core == 0, source[half:], source[:half])

    def pick(mask):
        return jnp.einsum(
            "ps,std->ptd", mask, tile_tokens, preferred_element_type=jnp.float32
        ).astype(jnp.bfloat16)

    given = pick(other_mask).reshape(half * tile_len, model_width)
    kept = pick(mine_mask).reshape(half * tile_len, model_width)
    chip_half = kept + swap_core(given)

    split = qkv_weight.reshape(rows_here, 3, HEADS, HD)
    send_weight = jnp.stack(
        [split[:, :, h : h + each].reshape(rows_here, 3 * wide) for h in first_head], axis=0
    )
    block = lax.all_to_all(send_weight, dev, split_axis=0, concat_axis=0, tiled=True)
    block = block.reshape(holders * rows_here, 3 * wide)
    group_rows = holders * rows_here
    weights = jnp.zeros((groups * group_rows, 3 * wide), jnp.bfloat16)
    weights = lax.dynamic_update_slice_in_dim(weights, block, group * group_rows, 0)
    for shift in range(1, groups):
        far = lax.ppermute(block, "grp", [(i, (i + shift) % groups) for i in range(groups)])
        weights = lax.dynamic_update_slice_in_dim(
            weights, far, ((group - shift) % groups) * group_rows, 0
        )

    canvas, send_weight = lax.optimization_barrier((canvas, send_weight))
    height, breadth = canvas.shape[0], canvas.shape[1]
    padded = with_halo(with_halo(canvas, "grp", 0), dev, 1)
    score_flat = conv_scores(padded, conv_weight, conv_bias, score_weight, height, breadth)
    score_map = score_flat.reshape(height, breadth)
    tile_score = jnp.take(score_flat, tile_cell[0]).astype(jnp.bfloat16)
    own_scores = jnp.sum(source.astype(jnp.float32) * tile_score.astype(jnp.float32), axis=1)
    held_score = sum_over_dev(own_scores, chips)
    sharpness = jnp.repeat(0.5 + jax.nn.softplus(held_score), tile_len)

    mixed = merge_project(chip_half, weights, ln_gain, chips, 8)
    queries = mixed[:, :wide].astype(jnp.bfloat16)
    keys = (mixed[:, wide : 2 * wide] * sharpness[:, None]).astype(jnp.bfloat16)
    values = mixed[:, 2 * wide :].astype(jnp.bfloat16)

    held_rows = MT * tile_len
    token_ids = jnp.repeat(tile_image[0], tile_len)

    def banded(value, fill):
        edge = [(held_rows, held_rows)] + [(0, 0)] * (value.ndim - 1)
        blocks = jnp.pad(value, edge, constant_values=fill)
        blocks = blocks.reshape((holders + 2, held_rows) + value.shape[1:])
        return jnp.concatenate([blocks[:-2], blocks[1:-1], blocks[2:]], axis=1)

    key_ids = banded(token_ids, -1)
    own_ids = token_ids.reshape(holders, held_rows)
    outs = []
    for head in range(each):
        lanes = slice(head * HD, (head + 1) * HD)
        outs.append(
            attend(
                queries[:, lanes].reshape(holders, held_rows, 1, HD),
                banded(keys[:, lanes], 0)[:, :, None],
                banded(values[:, lanes], 0)[:, :, None],
                own_ids,
                key_ids,
            )[:, :, 0]
        )
    mine = jnp.concatenate(outs, axis=2)
    heads_in = lax.all_to_all(mine, dev, split_axis=0, concat_axis=0, tiled=True)
    parts, done = [], 0
    for d in range(holders):
        if done < HEADS:
            skip = done - first_head[d]
            parts.append(heads_in[d][:, skip * HD :])
            done = first_head[d] + each
    return (score_map, jnp.concatenate(parts, axis=1))


def solution(mesh):
    groups, devs = mesh.devices.shape
    fine = Mesh(mesh.devices.reshape(groups, devs // 2, 2), ("grp", "chip", "core"))
    dev = ("chip", "core")
    every = ("grp", "chip", "core")
    placed = (
        P("grp", dev, None),
        P(),
        P(),
        P(),
        P(every, None, None),
        P("grp", dev),
        P("grp", None),
        P("grp", None),
        P("grp", None),
        P(),
        P(every, None),
    )
    return jax.shard_map(
        shards_by_head if devs == 8 else shards_by_core,
        mesh=fine,
        in_specs=placed,
        out_specs=(P("grp", dev), P(every, None)),
        check_vma=False,
    )
```
